128 devices in a mesh: dp: 2 (over core), ctx: 16 (over y, x), tp: 4 (over z).
Axes of the slice: x: 4, y: 4, z: 4, core: 2. Of those that a mesh axis runs over, the one named last changes fastest.
Arguments:
- queries: bfloat16 [4, 8192, 6144], P('dp', 'tp', 'ctx'), may hold values from -6 to 6
- key_proj: bfloat16 [4, 8192, 6144], P('dp', 'tp', 'ctx'), may hold values from -6 to 6
- value_proj: bfloat16 [4, 8192, 6144], P('dp', 'tp', 'ctx'), may hold values from -6 to 6
- grad_output: bfloat16 [4, 8192, 6144], P('dp', 'tp', 'ctx'), may hold values from -6 to 6
- filters: float32 [512, 128], P('tp'), may hold values from -0.5 to 0.5
- group_of: int32 [8192], P('tp'), may hold values from 0 to 511, as said below
Outputs:
- gated_out: bfloat16 [4, 8192, 6144], P('dp', 'tp', 'ctx')
- grad_queries: bfloat16 [4, 8192, 6144], P('dp', 'tp', 'ctx')
- grad_keys: bfloat16 [4, 8192, 6144], P('dp', 'tp', 'ctx')
- grad_values: bfloat16 [4, 8192, 6144], P('dp', 'tp', 'ctx')
- grad_filters: float32 [512, 128], P('tp')
The draws below stay inside these ranges and needn't reach their ends.
Inputs may be any that keep to these rules, and one draw needn't show every extreme that they name: `group_of`: channels come in aligned runs of 16 consecutive channels that share one filter row, and every filter row serves exactly one run.
All inputs are finite; a program needn't handle non-finite values.
Results may differ from the reference program's by a relative error of at most 0.0058.
Values may be sent and summed in bfloat16 or wider, within the bound.
A program may use at most 192 MiB of HBM per device.

```python
import jax
import jax.numpy as jnp
from jax import lax

D = 8192
GROUPS = 512
TAPS = 128
LENGTH = 6144
BATCH = 4
TOKENS = 24576


def draw_group_of(key, part):
    filter_order = jax.random.permutation(key, GROUPS)
    return jnp.repeat(filter_order, D // GROUPS).astype(jnp.int32)


def shard_levels(stream_key, dims, cuts, smallest, high):
    factor_of = 1.0
    for dim, parts in cuts:
        draws = jax.random.uniform(jax.random.fold_in(jax.random.fold_in(stream_key, 6), dim), (parts,), jnp.float32, smallest / len(cuts), high / len(cuts))
        factor_of = factor_of * jnp.repeat(jnp.exp(draws), dims[dim] // parts).reshape((-1,) + (1,) * (len(dims) - 1 - dim))
    return factor_of


def scatter_about(own_key, shape, spread, bound, pieces=(), kind=jnp.bfloat16):
    values = jax.random.normal(own_key, shape, jnp.float32) * spread
    if len(pieces) > 0:
        values = shard_levels(own_key, shape, pieces, -0.22, 0.18) * values
    return jnp.clip(values, min=-bound, max=bound).astype(kind)


def setup_inputs(seed: int = 0) -> dict:
    key_list = jax.random.split(jax.random.key(seed), 7)
    queries = scatter_about(key_list[0], (BATCH, D, LENGTH), 1.0, 6.0, ((0, 2), (1, 4), (2, 16)))
    key_proj = scatter_about(key_list[1], (BATCH, D, LENGTH), 1.0, 6.0, ((0, 2), (1, 4), (2, 16)))
    value_proj = scatter_about(key_list[2], (BATCH, D, LENGTH), 1.0, 6.0, ((0, 2), (1, 4), (2, 16)))
    grad_output = scatter_about(key_list[3], (BATCH, D, LENGTH), 1.0, 6.0, ((0, 2), (1, 4), (2, 16)))
    filters = scatter_about(key_list[4], (GROUPS, TAPS), TAPS ** -0.5, 0.5, ((0, 4),), jnp.float32)
    group_of = draw_group_of(jax.random.fold_in(key_list[6], 71), 0)
    return dict(queries=queries, key_proj=key_proj, value_proj=value_proj, grad_output=grad_output, filters=filters, group_of=group_of)


def reference(queries, key_proj, value_proj, grad_output, filters, group_of):
    wide = jnp.float32
    rounded = lax.optimization_barrier(filters.astype(jnp.bfloat16))
    filter_table = rounded.astype(wide)
    chan_taps_all = filter_table[group_of]
    block_width = min(D, 512)
    block_count = D // block_width
    fft_len = LENGTH + TAPS

    def one_window(window_pos):
        def select_row(array):
            return lax.dynamic_index_in_dim(array, window_pos, 0, keepdims=False)

        q_rows = select_row(queries)
        k_rows = select_row(key_proj)
        v_rows = select_row(value_proj)
        g_rows = select_row(grad_output)

        def one_block(block_pos):
            first_row = block_pos * block_width

            def cut_rows(array):
                return lax.dynamic_slice_in_dim(array, first_row, block_width, 0).astype(wide)

            q_block = cut_rows(q_rows)
            k_block = cut_rows(k_rows)
            v_block = cut_rows(v_rows)
            g_block = cut_rows(g_rows)
            chan_taps = lax.dynamic_slice_in_dim(chan_taps_all, first_row, block_width, 0)
            product = lax.optimization_barrier((k_block * v_block).astype(jnp.bfloat16)).astype(wide)
            backward = lax.optimization_barrier((g_block * q_block).astype(jnp.bfloat16)).astype(wide)
            spec_prod = jnp.fft.rfft(product, n=fft_len, axis=1)
            spec_taps = jnp.fft.rfft(chan_taps, n=fft_len, axis=1)
            spec_back = jnp.fft.rfft(backward, n=fft_len, axis=1)
            mixed_rows = jnp.fft.irfft(spec_prod * spec_taps, n=fft_len, axis=1)[:, :LENGTH].astype(wide)
            upward = jnp.fft.irfft(spec_back * jnp.conj(spec_taps), n=fft_len, axis=1)[:, :LENGTH].astype(wide)
            tap_grad = jnp.fft.irfft(spec_back * jnp.conj(spec_prod), n=fft_len, axis=1)[:, :TAPS].astype(wide)
            return ((q_block * mixed_rows).astype(jnp.bfloat16),
                    (g_block * mixed_rows).astype(jnp.bfloat16),
                    (upward * v_block).astype(jnp.bfloat16),
                    (upward * k_block).astype(jnp.bfloat16),
                    tap_grad)

        results = lax.map(one_block, jnp.arange(block_count, dtype=jnp.int32))

        def join_rows(stacked):
            return stacked.reshape(D, LENGTH)

        chan_grad = results[4].reshape(D, TAPS)
        return (join_rows(results[0]), join_rows(results[1]), join_rows(results[2]), join_rows(results[3]), chan_grad)

    gated_out, grad_queries, grad_keys, grad_values, chan_grads = lax.map(one_window, jnp.arange(BATCH, dtype=jnp.int32))
    summed = jnp.sum(chan_grads, axis=0)
    grad_filters = jax.ops.segment_sum(summed, group_of, num_segments=GROUPS) / TOKENS
    return gated_out, grad_queries, grad_keys, grad_values, grad_filters
```

```python
import jax
import jax.numpy as jnp
from jax import lax
from jax.experimental import pallas as pl
from jax.experimental.pallas import tpu as pltpu
from jax.sharding import PartitionSpec as P

BF16 = jnp.bfloat16
F32 = jnp.float32
TAPS = 128
MEMBERS = 16
GROUPS = 512
CHUNKS = 16
AHEAD = 3
FIRST = 8
MESH = pl.DeviceIdType.MESH


def aligned(index, size):
    return pl.ds(pl.multiple_of(index * size, size), size)


def shards(queries, key_proj, value_proj, grad_output, filters, group_of, tokens, nx):
    windows, channels, positions = queries.shape
    runs = channels // MEMBERS
    blocks = positions // TAPS
    width = channels // CHUNKS
    chunk_runs = width // MEMBERS
    stack = windows * MEMBERS
    half = runs // 2
    ctx_size = lax.axis_size("ctx")
    tp_size = lax.axis_size("tp")
    ny = ctx_size // nx
    scale_by = 1.0 / tokens

    def body(
        filt_ref, grp_ref, q_hbm, k_hbm, v_hbm, g_hbm,
        gated, gradq, gradk, gradv, gradf,
        q, k, v, g, u_out, d_out, u_in, d_in, circs, masks, table, groups, taps_of,
        partial, local, core_in, y_all, x_all, whole, z_all,
        edge_sem, rest_sem, halo_send, halo_recv, table_send, table_recv,
        core_send, core_recv, y_send, y_recv, x_send, x_recv, z_send, z_recv,
    ):
        dp = lax.axis_index("dp")
        ctx = lax.axis_index("ctx")
        tp = lax.axis_index("tp")
        y = ctx // nx
        x = lax.rem(ctx, nx)
        after = {"ctx": lax.rem(ctx + 1, ctx_size)}
        before = {"ctx": lax.rem(ctx + ctx_size - 1, ctx_size)}
        other = {"dp": 1 - dp}
        y_peers = [{"ctx": lax.rem(y + i, ny) * nx + x} for i in range(1, ny)]
        x_peers = [{"ctx": y * nx + lax.rem(x + i, nx)} for i in range(1, nx)]
        z_peers = [{"tp": lax.rem(tp + i, tp_size)} for i in range(1, tp_size)]
        peers = [after, before] + z_peers + x_peers + y_peers + [other]
        barrier = pltpu.get_barrier_semaphore()
        for peer in peers:
            pl.semaphore_signal(barrier, 1, device_id=peer, device_id_type=MESH)

        hbm = [k_hbm, v_hbm, q_hbm, g_hbm]
        vmem = [k, v, q, g]
        edge_lane = [positions - TAPS, positions - TAPS, 0, 0]
        rest_lane = [0, 0, TAPS, TAPS]
        pieces = 4
        piece = channels // pieces

        def edge_copy(a, p):
            part = (slice(None), pl.ds(p * piece, piece), pl.ds(edge_lane[a], TAPS))
            return pltpu.make_async_copy(hbm[a].at[part], vmem[a].at[part], edge_sem.at[a, p])

        def rest_copy(a, c):
            part = (slice(None), aligned(c, width), pl.ds(rest_lane[a], positions - TAPS))
            return pltpu.make_async_copy(hbm[a].at[part], vmem[a].at[part], rest_sem.at[a, c])

        for p in range(pieces):
            for a, at in ((0, p), (1, p), (2, pieces - 1 - p), (3, pieces - 1 - p)):
                edge_copy(a, at).start()

        def start_rest(i, carry):
            for a in range(4):
                rest_copy(a, i).start()
                rest_copy(a, CHUNKS - 1 - i).start()
            return carry

        lax.fori_loop(0, CHUNKS // 2, start_rest, 0)

        row = lax.broadcasted_iota(jnp.int32, (TAPS, TAPS), 0)
        lane = lax.broadcasted_iota(jnp.int32, (TAPS, TAPS), 1)
        masks[0] = jnp.where(lane >= row, 1.0, 0.0).astype(BF16)
        masks[1] = jnp.where(lane < row, 1.0, 0.0).astype(BF16)
        table[tp] = filt_ref[...].astype(BF16)
        groups[tp] = grp_ref[...]
        has_after = jnp.where(ctx < ctx_size - 1, 1.0, 0.0).astype(F32)
        has_before = jnp.where(ctx > 0, 1.0, 0.0).astype(F32)

        for p in range(pieces):
            at = pieces - 1 - p
            edge_copy(0, p).wait()
            edge_copy(1, p).wait()
            ch = pl.ds(p * piece, piece)
            ln = pl.ds(positions - TAPS, TAPS)
            scaled = k[:, ch, ln].astype(F32) * v[:, ch, ln].astype(F32) * has_after
            u_out[:, ch, :] = scaled.astype(BF16)
            edge_copy(2, at).wait()
            edge_copy(3, at).wait()
            ch = pl.ds(at * piece, piece)
            ln = pl.ds(0, TAPS)
            scaled = q[:, ch, ln].astype(F32) * g[:, ch, ln].astype(F32) * has_before
            d_out[:, ch, :] = scaled.astype(BF16)

        pl.semaphore_wait(barrier, len(peers))

        def u_copy(c):
            part = (slice(None), aligned(c, width), slice(None))
            return pltpu.make_async_remote_copy(
                u_out.at[part], u_in.at[part], halo_send.at[0, c], halo_recv.at[0, c],
                device_id=after, device_id_type=MESH,
            )

        def d_copy(c):
            part = (slice(None), aligned(c, width), slice(None))
            return pltpu.make_async_remote_copy(
                d_out.at[part], d_in.at[part], halo_send.at[1, c], halo_recv.at[1, c],
                device_id=before, device_id_type=MESH,
            )

        def start_halo(i):
            u_copy(i).start()
            d_copy(CHUNKS - 1 - i).start()

        start_halo(0)

        def table_copies(i):
            return [
                pltpu.make_async_remote_copy(
                    ref.at[tp], ref.at[tp], table_send.at[j, i], table_recv.at[j, i],
                    device_id=z_peers[i], device_id_type=MESH,
                )
                for j, ref in enumerate((table, groups))
            ]

        for i in range(tp_size - 1):
            for copy in table_copies(i):
                copy.start()

        def start_more(i, carry):
            start_halo(i)
            return carry

        lax.fori_loop(1, FIRST, start_more, 0)

        def advance(step):
            @pl.when(jnp.logical_and(step + AHEAD >= FIRST, step + AHEAD < CHUNKS))
            def _():
                start_halo(step + AHEAD)

        for i in range(tp_size - 1):
            for copy in table_copies(i):
                copy.wait()

        def run_groups(z):
            ids = groups[z]
            span = TAPS // MEMBERS
            pick = jnp.where(
                lax.broadcasted_iota(jnp.int32, (runs, channels // TAPS), 1)
                == lax.broadcasted_iota(jnp.int32, (runs, channels // TAPS), 0) // span,
                1.0, 0.0,
            ).astype(BF16)
            high = jnp.dot(pick, (ids >> 4).astype(F32).astype(BF16), preferred_element_type=F32)
            low = jnp.dot(pick, (ids & 15).astype(F32).astype(BF16), preferred_element_type=F32)
            r = lax.broadcasted_iota(jnp.int32, (runs, TAPS), 0)
            l = lax.broadcasted_iota(jnp.int32, (runs, TAPS), 1)
            keep = jnp.where(l == (r % span) * MEMBERS, high * 16.0 + low, 0.0)
            return jnp.sum(keep, axis=1, keepdims=True)

        mine = run_groups(tp)
        rows_here = GROUPS // tp_size
        chosen = jnp.zeros((runs, TAPS), F32)
        for z in range(tp_size):
            ids = lax.broadcasted_iota(jnp.int32, (runs, rows_here), 1) + z * rows_here
            onehot = jnp.where(ids.astype(F32) == mine, 1.0, 0.0).astype(BF16)
            chosen = chosen + jnp.dot(onehot, table[z], preferred_element_type=F32)
        taps_of[...] = chosen

        nothing = jnp.zeros((stack, TAPS), BF16)

        def run_rows(ref, r, b):
            return jnp.concatenate(
                [ref[w, aligned(r, MEMBERS), TAPS * b : TAPS * b + TAPS] for w in range(windows)], axis=0
            )

        def product(left, right, r):
            return [run_rows(left, r, b) * run_rows(right, r, b) for b in range(blocks)]

        def put(out, gate, r, value):
            for b in range(blocks):
                for w in range(windows):
                    at = (w, aligned(r, MEMBERS), slice(TAPS * b, TAPS * b + TAPS))
                    first = b * stack + w * MEMBERS
                    out[at] = (gate[at].astype(F32) * value[first : first + MEMBERS]).astype(BF16)

        def circulant(r):
            rows = jnp.broadcast_to(taps_of[pl.ds(r, 1), :], (TAPS, TAPS))
            made = pltpu.roll(rows, 0, 1, stride=1, stride_axis=0).astype(BF16)
            circs[r] = made
            return made

        def outer(u_four, d_four, r):
            left = jnp.concatenate(u_four, axis=0)
            shifted = [nothing] + d_four
            right = jnp.concatenate(
                [jnp.concatenate([shifted[i + 1], shifted[i]], axis=1) for i in range(blocks + 1)], axis=0
            )
            pairs = lax.dot_general(left, right, (((0,), (0,)), ((), ())), preferred_element_type=F32)
            folded = jnp.where(lane >= row, pairs[:, TAPS:], pairs[:, :TAPS])
            total = folded[0:8]
            for i in range(1, TAPS // 8):
                total = total + pltpu.roll(folded[8 * i : 8 * i + 8], TAPS - 8 * i, 1)
            partial[aligned(r, 8), :] = total

        def forward(u_four, circ, r):
            weights = jnp.concatenate([circ * masks[1], circ * masks[0]], axis=0)
            left = jnp.concatenate(
                [jnp.concatenate([u_four[b], u_four[b + 1]], axis=1) for b in range(blocks)], axis=0
            )
            mixed = jnp.dot(left, weights, preferred_element_type=F32)
            put(gated, q, r, mixed)
            put(gradq, g, r, mixed)

        def backward(d_four, circ, r):
            weights = jnp.concatenate([circ * masks[0], circ * masks[1]], axis=1)
            left = jnp.concatenate(
                [jnp.concatenate([d_four[b], d_four[b + 1]], axis=1) for b in range(blocks)], axis=0
            )
            upward = lax.dot_general(left, weights, (((1,), (1,)), ((), ())), preferred_element_type=F32)
            put(gradk, v, r, upward)
            put(gradv, k, r, upward)

        def front_first(r):
            circ = circulant(r)
            u_four = [run_rows(u_in, r, 0)] + product(k, v, r)
            outer(u_four, product(g, q, r) + [nothing], r)
            forward(u_four, circ, r)

        def back_first(r):
            circ = circulant(r)
            d_four = product(g, q, r) + [run_rows(d_in, r, 0)]
            outer([nothing] + product(k, v, r), d_four, r)
            backward(d_four, circ, r)

        unroll = 4

        def first_phase(step, carry):
            back = CHUNKS - 1 - step
            for a in range(4):
                rest_copy(a, step).wait()
                rest_copy(a, back).wait()
            u_copy(step).wait_recv()
            d_copy(back).wait_recv()
            advance(step)

            def some(i, inner):
                for j in range(unroll):
                    front_first(step * chunk_runs + i * unroll + j)
                    back_first(back * chunk_runs + i * unroll + j)
                return inner

            return lax.fori_loop(0, chunk_runs // unroll, some, carry)

        lax.fori_loop(0, CHUNKS // 2, first_phase, 0)

        def second_phase(step, carry):
            back = CHUNKS - 1 - step
            u_copy(step).wait_recv()
            d_copy(back).wait_recv()
            advance(step)

            def some(i, inner):
                for j in range(unroll):
                    r = step * chunk_runs + i * unroll + j
                    forward([run_rows(u_in, r, 0)] + product(k, v, r), circs[r], r)
                    r = back * chunk_runs + i * unroll + j
                    backward(product(g, q, r) + [run_rows(d_in, r, 0)], circs[r], r)
                return inner

            return lax.fori_loop(0, chunk_runs // unroll, some, carry)

        total = partial[pl.ds(0, runs, stride=8), :]
        for s in range(1, 8):
            total = total + pltpu.roll(partial[pl.ds(s, runs, stride=8), :], TAPS - s, 1)
        local[...] = total
        own = aligned(dp, half)
        theirs = aligned(1 - dp, half)
        core_copy = pltpu.make_async_remote_copy(
            local.at[theirs], core_in, core_send.at[0], core_recv.at[0], device_id=other, device_id_type=MESH
        )
        core_copy.start()
        middle = CHUNKS // 2
        lax.fori_loop(middle, middle + 1, second_phase, 0)

        def spread(ref, slot, send, recv, to):
            return [
                pltpu.make_async_remote_copy(
                    ref.at[slot], ref.at[slot], send.at[i], recv.at[i], device_id=peer, device_id_type=MESH
                )
                for i, peer in enumerate(to)
            ]

        core_copy.wait()
        y_all[y] = local[own, :] + core_in[...]
        y_copies = spread(y_all, y, y_send, y_recv, y_peers)
        for copy in y_copies:
            copy.start()
        lax.fori_loop(middle + 1, middle + 3, second_phase, 0)
        for copy in y_copies:
            copy.wait()
        summed = y_all[0]
        for i in range(1, ny):
            summed = summed + y_all[i]
        x_all[x] = summed
        x_copies = spread(x_all, x, x_send, x_recv, x_peers)
        for copy in x_copies:
            copy.start()
        lax.fori_loop(middle + 3, middle + 6, second_phase, 0)
        for copy in x_copies:
            copy.wait()
        summed = x_all[0]
        for i in range(1, nx):
            summed = summed + x_all[i]
        z_all[tp, own, :] = summed
        core_back = pltpu.make_async_remote_copy(
            z_all.at[tp, own, :], z_all.at[tp, own, :], core_send.at[1], core_recv.at[1],
            device_id=other, device_id_type=MESH,
        )
        core_back.start()
        lax.fori_loop(middle + 6, middle + 7, second_phase, 0)
        core_back.wait()
        z_copies = spread(z_all, tp, z_send, z_recv, z_peers)
        for copy in z_copies:
            copy.start()
        lax.fori_loop(middle + 7, middle + 8, second_phase, 0)
        for copy in z_copies:
            copy.wait()
        result = jnp.zeros((rows_here, TAPS), F32)
        first_row = tp * rows_here
        for z in range(tp_size):
            ids = lax.broadcasted_iota(jnp.int32, (runs, rows_here), 1) + first_row
            onehot = jnp.where(ids.astype(F32) == run_groups(z), 1.0, 0.0).astype(BF16)
            rest = z_all[z]
            for _ in range(3):
                piece_of = rest.astype(BF16)
                rest = rest - piece_of.astype(F32)
                result = result + lax.dot_general(
                    onehot, piece_of, (((0,), (0,)), ((), ())), preferred_element_type=F32
                )
        gradf[...] = result * scale_by

        def finish(i, carry):
            u_copy(i).wait_send()
            d_copy(i).wait_send()
            return carry

        lax.fori_loop(0, CHUNKS, finish, 0)

    resident = pl.BlockSpec(memory_space=pltpu.VMEM)
    remote = pl.BlockSpec(memory_space=pltpu.HBM)
    big = (windows, channels, positions)
    halo = (windows, channels, TAPS)
    dma = pltpu.SemaphoreType.DMA
    results = pl.pallas_call(
        body,
        out_shape=[pltpu.VMEM(big, BF16)] * 4 + [jax.ShapeDtypeStruct((GROUPS // tp_size, TAPS), F32)],
        in_specs=[resident, resident] + [remote] * 4,
        out_specs=[resident] * 5,
        scratch_shapes=[pltpu.VMEM(big, BF16)] * 4
        + [pltpu.VMEM(halo, BF16)] * 4
        + [
            pltpu.VMEM((runs, TAPS, TAPS), BF16),
            pltpu.VMEM((2, TAPS, TAPS), BF16),
            pltpu.VMEM((tp_size, GROUPS // tp_size, TAPS), BF16),
            pltpu.VMEM((tp_size, channels // TAPS, TAPS), jnp.int32),
            pltpu.VMEM((runs, TAPS), F32),
            pltpu.VMEM((runs * 8, TAPS), F32),
            pltpu.VMEM((runs, TAPS), F32),
            pltpu.VMEM((half, TAPS), F32),
            pltpu.VMEM((ny, half, TAPS), F32),
            pltpu.VMEM((nx, half, TAPS), F32),
            pltpu.VMEM((8, TAPS), F32),
            pltpu.VMEM((tp_size, runs, TAPS), F32),
            dma((4, 4)), dma((4, CHUNKS)), dma((2, CHUNKS)), dma((2, CHUNKS)), dma((2, tp_size - 1)), dma((2, tp_size - 1)),
            dma((2,)), dma((2,)), dma((ny - 1,)), dma((ny - 1,)), dma((nx - 1,)), dma((nx - 1,)),
            dma((tp_size - 1,)), dma((tp_size - 1,)),
        ],
        compiler_params=pltpu.CompilerParams(collective_id=0, has_side_effects=True, vmem_limit_bytes=42 << 20),
    )(filters, group_of.reshape(channels // TAPS, TAPS), queries, key_proj, value_proj, grad_output)

    def write(*refs):
        ins, outs, sem = refs[:4], refs[4:8], refs[8]
        copies = [
            pltpu.make_async_copy(ins[a].at[w], outs[a].at[w], sem.at[a, w])
            for a in range(4)
            for w in range(windows)
        ]
        for copy in copies:
            copy.start()
        for copy in copies:
            copy.wait()

    held = [pltpu.with_memory_space_constraint(r, pltpu.VMEM) for r in results[:4]]
    written = pl.pallas_call(
        write,
        out_shape=[jax.ShapeDtypeStruct(big, BF16)] * 4,
        in_specs=[resident] * 4,
        out_specs=[remote] * 4,
        scratch_shapes=[dma((4, windows))],
        compiler_params=pltpu.CompilerParams(vmem_limit_bytes=4 << 20),
    )(*held)
    return (*written, results[4])


def solution(mesh):
    spec = P("dp", "tp", "ctx")
    nx = 4

    def call(queries, key_proj, value_proj, grad_output, filters, group_of):
        tokens = queries.shape[0] * queries.shape[2]

        def local(*args):
            return shards(*args, tokens, nx)

        return jax.shard_map(
            local,
            mesh=mesh,
            in_specs=(spec, spec, spec, spec, P("tp", None), P("tp")),
            out_specs=(spec, spec, spec, spec, P("tp", None)),
            check_vma=False,
        )(queries, key_proj, value_proj, grad_output, filters, group_of)

    return call
```

```python
import jax
import jax.numpy as jnp
from jax import lax
from jax.experimental import pallas as pl
from jax.experimental.pallas import tpu as pltpu
from jax.sharding import PartitionSpec as P

BF16 = jnp.bfloat16
F32 = jnp.float32
TAPS = 128
MEMBERS = 16
GROUPS = 512
CHUNKS = 16
EARLY = 2
LATER = 5
EDGES = (0, 1, 4, 8, 16)
PARTS = 1
STEPS = (1, 8)
MESH = pl.DeviceIdType.MESH


def aligned(index, size):
    return pl.ds(pl.multiple_of(index * size, size), size)


def shards(queries, key_proj, value_proj, grad_output, filters, group_of, tokens, nx):
    windows, channels, positions = queries.shape
    runs = channels // MEMBERS
    blocks = positions // TAPS
    width = channels // CHUNKS
    chunk_runs = width // MEMBERS
    stack = windows * MEMBERS
    half = runs // 2
    ctx_size = lax.axis_size("ctx")
    tp_size = lax.axis_size("tp")
    ny = ctx_size // nx
    scale_by = 1.0 / tokens

    def body(
        filt_ref, grp_ref, q_hbm, k_hbm, v_hbm, g_hbm,
        gated, gradq, gradk, gradv, gradf,
        q, k, v, g, u_out, d_out, u_in, d_in, masks, table, groups, taps_of, routes,
        partial, local, core_in, y_all, x_all, z_all, routed, both,
        edge_sem, rest_sem, halo_send, halo_recv, table_send, table_recv,
        known, core_send, core_recv, y_send, y_recv, x_send, x_recv, z_send, z_recv, last_send, last_recv,
    ):
        dp = lax.axis_index("dp")
        ctx = lax.axis_index("ctx")
        tp = lax.axis_index("tp")
        y = ctx // nx
        x = lax.rem(ctx, nx)
        after = {"ctx": lax.rem(ctx + 1, ctx_size)}
        before = {"ctx": lax.rem(ctx + ctx_size - 1, ctx_size)}
        other = {"dp": 1 - dp}
        y_peers = [{"ctx": lax.rem(y + i, ny) * nx + x} for i in range(1, ny)]
        x_peers = [{"ctx": y * nx + lax.rem(x + i, nx)} for i in range(1, nx)]
        z_peers = [{"tp": lax.rem(tp + i, tp_size)} for i in range(1, tp_size)]
        last_peers = [other] + z_peers + [{"dp": 1 - dp, **peer} for peer in z_peers]
        greeted = [after, before, other] + z_peers
        barrier = pltpu.get_barrier_semaphore()
        for peer in greeted:
            pl.semaphore_signal(barrier, 1, device_id=peer, device_id_type=MESH)

        def along(distance):
            return {"ctx": lax.rem(ctx + distance + ctx_size, ctx_size)}

        def pass_on(round_of, to):
            for peer in to:
                pl.semaphore_signal(known.at[round_of], 1, device_id=peer, device_id_type=MESH)

        hbm = [k_hbm, v_hbm, q_hbm, g_hbm]
        vmem = [k, v, q, g]
        edge_lane = [positions - TAPS, positions - TAPS, 0, 0]
        rest_lane = [0, 0, TAPS, TAPS]
        pieces = len(EDGES) - 1

        def edge_rows(a, p):
            low, high = EDGES[p] * width, EDGES[p + 1] * width
            return pl.ds(low, high - low) if a < 2 else pl.ds(channels - high, high - low)

        def edge_copy(a, p):
            part = (slice(None), edge_rows(a, p), pl.ds(edge_lane[a], TAPS))
            return pltpu.make_async_copy(hbm[a].at[part], vmem[a].at[part], edge_sem.at[a, p])

        def rest_copy(a, c):
            part = (slice(None), aligned(c, width), pl.ds(rest_lane[a], positions - TAPS))
            return pltpu.make_async_copy(hbm[a].at[part], vmem[a].at[part], rest_sem.at[a, c])

        for p in range(pieces):
            for a in range(4):
                edge_copy(a, p).start()

        def start_rest(i, carry):
            for a in range(4):
                rest_copy(a, i).start()
                rest_copy(a, CHUNKS - 1 - i).start()
            return carry

        def u_copy(c):
            part = (slice(None), aligned(c, width), slice(None))
            return pltpu.make_async_remote_copy(
                u_out.at[part], u_in.at[part], halo_send.at[0, c], halo_recv.at[0, c],
                device_id=after, device_id_type=MESH,
            )

        def d_copy(c):
            part = (slice(None), aligned(c, width), slice(None))
            return pltpu.make_async_remote_copy(
                d_out.at[part], d_in.at[part], halo_send.at[1, c], halo_recv.at[1, c],
                device_id=before, device_id_type=MESH,
            )

        not_first = ctx > 0
        not_last = ctx < ctx_size - 1

        def start_halo(i, carry):
            @pl.when(not_last)
            def _():
                u_copy(i).start()

            @pl.when(not_first)
            def _():
                d_copy(CHUNKS - 1 - i).start()

            return carry

        def halo_here(step):
            @pl.when(not_first)
            def _():
                u_copy(step).wait_recv()

            @pl.when(not_last)
            def _():
                d_copy(CHUNKS - 1 - step).wait_recv()

        def table_copies(i):
            return [
                pltpu.make_async_remote_copy(
                    ref.at[tp], ref.at[tp], table_send.at[j, i], table_recv.at[j, i],
                    device_id=z_peers[i], device_id_type=MESH,
                )
                for j, ref in enumerate((table, groups))
            ]

        @pl.when(ctx == 0)
        def _():
            u_in[...] = jnp.zeros_like(u_in)

        @pl.when(ctx == ctx_size - 1)
        def _():
            d_in[...] = jnp.zeros_like(d_in)

        for p in range(pieces):
            edge_copy(0, p).wait()
            edge_copy(1, p).wait()
            ch, ln = edge_rows(0, p), pl.ds(positions - TAPS, TAPS)
            u_out[:, ch, :] = k[:, ch, ln] * v[:, ch, ln]
            edge_copy(2, p).wait()
            edge_copy(3, p).wait()
            ch, ln = edge_rows(2, p), pl.ds(0, TAPS)
            d_out[:, ch, :] = q[:, ch, ln] * g[:, ch, ln]
            if p == 0:
                pl.semaphore_wait(barrier, len(greeted))
            lax.fori_loop(EDGES[p], EDGES[p + 1], start_halo, 0)
            if p == 0:
                table[tp] = filt_ref[...].astype(BF16)
                groups[tp] = grp_ref[...]
                for i in range(tp_size - 1):
                    for copy in table_copies(i):
                        copy.start()
                pass_on(0, [after, before, other])
            if p == 1:
                lax.fori_loop(0, CHUNKS // 2, start_rest, 0)

        row = lax.broadcasted_iota(jnp.int32, (TAPS, TAPS), 0)
        lane = lax.broadcasted_iota(jnp.int32, (TAPS, TAPS), 1)
        masks[0] = jnp.where(lane >= row, 1.0, 0.0).astype(BF16)
        masks[1] = jnp.where(lane < row, 1.0, 0.0).astype(BF16)

        nothing = jnp.zeros((stack, TAPS), BF16)

        def run_rows(ref, r, b):
            return jnp.concatenate(
                [ref[w, aligned(r, MEMBERS), TAPS * b : TAPS * b + TAPS] for w in range(windows)], axis=0
            )

        def product(left, right, r):
            return [run_rows(left, r, b) * run_rows(right, r, b) for b in range(blocks)]

        def put(out, gate, r, value):
            for b in range(blocks):
                for w in range(windows):
                    at = (w, aligned(r, MEMBERS), slice(TAPS * b, TAPS * b + TAPS))
                    first = b * stack + w * MEMBERS
                    out[at] = (gate[at].astype(F32) * value[first : first + MEMBERS]).astype(BF16)

        def circulant(r):
            rows = jnp.broadcast_to(taps_of[pl.ds(r, 1), :], (TAPS, TAPS))
            return pltpu.roll(rows, 0, 1, stride=1, stride_axis=0).astype(BF16)

        def outer(u_four, d_four, r):
            left = jnp.concatenate(u_four, axis=0)
            shifted = [nothing] + d_four
            right = jnp.concatenate(
                [jnp.concatenate([shifted[i + 1], shifted[i]], axis=1) for i in range(blocks + 1)], axis=0
            )
            pairs = lax.dot_general(left, right, (((0,), (0,)), ((), ())), preferred_element_type=F32)
            folded = jnp.where(lane >= row, pairs[:, TAPS:], pairs[:, :TAPS])
            total = folded[0:8]
            for i in range(1, TAPS // 8):
                total = total + pltpu.roll(folded[8 * i : 8 * i + 8], TAPS - 8 * i, 1)
            partial[aligned(r, 8), :] = total

        def forward(r):
            circ = circulant(r)
            u_four = [run_rows(u_in, r, 0)] + product(k, v, r)
            weights = jnp.concatenate([circ * masks[1], circ * masks[0]], axis=0)
            left = jnp.concatenate(
                [jnp.concatenate([u_four[b], u_four[b + 1]], axis=1) for b in range(blocks)], axis=0
            )
            mixed = jnp.dot(left, weights, preferred_element_type=F32)
            put(gated, q, r, mixed)
            put(gradq, g, r, mixed)

        def backward(r):
            circ = circulant(r)
            d_four = product(g, q, r) + [run_rows(d_in, r, 0)]
            weights = jnp.concatenate([circ * masks[0], circ * masks[1]], axis=1)
            left = jnp.concatenate(
                [jnp.concatenate([d_four[b], d_four[b + 1]], axis=1) for b in range(blocks)], axis=0
            )
            upward = lax.dot_general(left, weights, (((1,), (1,)), ((), ())), preferred_element_type=F32)
            put(gradk, v, r, upward)
            put(gradv, k, r, upward)

        unroll = 4

        def first_phase(step, carry):
            back = CHUNKS - 1 - step
            for a in range(4):
                rest_copy(a, step).wait()
                rest_copy(a, back).wait()
            halo_here(step)

            def some(i, inner):
                for j in range(unroll):
                    r = step * chunk_runs + i * unroll + j
                    outer([run_rows(u_in, r, 0)] + product(k, v, r), product(g, q, r) + [nothing], r)
                    r = back * chunk_runs + i * unroll + j
                    outer([nothing] + product(k, v, r), product(g, q, r) + [run_rows(d_in, r, 0)], r)
                return inner

            lax.fori_loop(0, chunk_runs // unroll, some, 0)
            for c in (step, back):
                first = pl.multiple_of(c * chunk_runs * 8, chunk_runs * 8)
                total = partial[pl.ds(first, chunk_runs, stride=8), :]
                for s in range(1, 8):
                    total = total + pltpu.roll(partial[pl.ds(first + s, chunk_runs, stride=8), :], TAPS - s, 1)
                local[aligned(c, chunk_runs), :] = total
            return carry

        middle = CHUNKS // 2
        lax.fori_loop(0, EARLY, first_phase, 0)

        pl.semaphore_wait(known.at[0], 3)
        pass_on(1, [along(2), along(-2)])
        for i in range(tp_size - 1):
            for copy in table_copies(i):
                copy.wait()

        def run_groups(z):
            ids = groups[z]
            span = TAPS // MEMBERS
            pick = jnp.where(
                lax.broadcasted_iota(jnp.int32, (runs, channels // TAPS), 1)
                == lax.broadcasted_iota(jnp.int32, (runs, channels // TAPS), 0) // span,
                1.0, 0.0,
            ).astype(BF16)
            high = jnp.dot(pick, (ids >> 4).astype(F32).astype(BF16), preferred_element_type=F32)
            low = jnp.dot(pick, (ids & 15).astype(F32).astype(BF16), preferred_element_type=F32)
            r = lax.broadcasted_iota(jnp.int32, (runs, TAPS), 0)
            l = lax.broadcasted_iota(jnp.int32, (runs, TAPS), 1)
            keep = jnp.where(l == (r % span) * MEMBERS, high * 16.0 + low, 0.0)
            return jnp.sum(keep, axis=1, keepdims=True)

        mine = run_groups(tp)
        rows_here = GROUPS // tp_size
        chosen = jnp.zeros((runs, TAPS), F32)
        for z in range(tp_size):
            ids = lax.broadcasted_iota(jnp.int32, (runs, rows_here), 1) + z * rows_here
            onehot = jnp.where(ids.astype(F32) == mine, 1.0, 0.0).astype(BF16)
            chosen = chosen + jnp.dot(onehot, table[z], preferred_element_type=F32)
        taps_of[...] = chosen
        first_row = tp * rows_here
        for z in range(tp_size):
            ids = lax.broadcasted_iota(jnp.int32, (runs, rows_here), 1) + first_row
            onehot = jnp.where(ids.astype(F32) == run_groups(z), 1.0, 0.0)
            routes[:, runs * z : runs * (z + 1)] = onehot.T.astype(BF16)

        lax.fori_loop(EARLY, LATER, first_phase, 0)
        pl.semaphore_wait(known.at[1], 2)
        pass_on(2, [along(4), along(-4)])
        lax.fori_loop(LATER, middle, first_phase, 0)
        pl.semaphore_wait(known.at[2], 2)

        def second_phase(step, carry):
            back = CHUNKS - 1 - step

            @pl.when(step >= middle)
            def _():
                halo_here(step)

            def some(i, inner):
                for j in range(unroll):
                    forward(step * chunk_runs + i * unroll + j)
                    backward(back * chunk_runs + i * unroll + j)
                return inner

            return lax.fori_loop(0, chunk_runs // unroll, some, carry)

        own = aligned(dp, half)
        theirs = aligned(1 - dp, half)
        core_copy = pltpu.make_async_remote_copy(
            local.at[theirs], core_in, core_send, core_recv, device_id=other, device_id_type=MESH
        )
        core_copy.start()
        def finish(i, carry):
            @pl.when(not_last)
            def _():
                u_copy(i).wait_send()

            @pl.when(not_first)
            def _():
                d_copy(i).wait_send()

            return carry

        lax.fori_loop(0, STEPS[0], second_phase, 0)

        def spread(ref, slot, send, recv, to):
            copies = [
                pltpu.make_async_remote_copy(
                    ref.at[slot], ref.at[slot], send.at[i], recv.at[i], device_id=peer, device_id_type=MESH
                )
                for i, peer in enumerate(to)
            ]
            for copy in copies:
                copy.start()
            return copies

        def summed(ref, count):
            result = ref[0]
            for i in range(1, count):
                result = result + ref[i]
            return result

        core_copy.wait()
        z_all[tp, dp] = local[own, :] + core_in[...]
        z_copies = spread(z_all, (tp, dp), z_send, z_recv, last_peers)
        lax.fori_loop(STEPS[0], STEPS[1], second_phase, 0)
        for copy in z_copies:
            copy.wait()
        rest = jnp.concatenate([z_all[z, core] for z in range(tp_size) for core in range(2)], axis=0)
        result = jnp.zeros((rows_here, TAPS), F32)
        for _ in range(3):
            piece_of = rest.astype(BF16)
            rest = rest - piece_of.astype(F32)
            result = result + jnp.dot(routes[...], piece_of, preferred_element_type=F32)
        routed[...] = result * scale_by
        x_all[x] = routed[own, :]
        x_copies = spread(x_all, x, x_send, x_recv, x_peers)
        lax.fori_loop(STEPS[1], CHUNKS, second_phase, 0)
        for copy in x_copies:
            copy.wait()
        y_all[y] = summed(x_all, nx)
        y_copies = spread(y_all, y, y_send, y_recv, y_peers)
        lax.fori_loop(0, CHUNKS, finish, 0)
        for copy in y_copies:
            copy.wait()
        both[dp] = summed(y_all, ny)
        last_copy = pltpu.make_async_remote_copy(
            both.at[dp], both.at[dp], last_send, last_recv, device_id=other, device_id_type=MESH
        )
        last_copy.start()
        last_copy.wait()
        gradf[: rows_here // 2, :] = both[0]
        gradf[rows_here // 2 :, :] = both[1]


    resident = pl.BlockSpec(memory_space=pltpu.VMEM)
    remote = pl.BlockSpec(memory_space=pltpu.HBM)
    big = (windows, channels, positions)
    halo = (windows, channels, TAPS)
    dma = pltpu.SemaphoreType.DMA
    results = pl.pallas_call(
        body,
        out_shape=[pltpu.VMEM(big, BF16)] * 4 + [pltpu.VMEM((GROUPS // tp_size, TAPS), F32)],
        in_specs=[resident, resident] + [remote] * 4,
        out_specs=[resident] * 5,
        scratch_shapes=[pltpu.VMEM(big, BF16)] * 4
        + [pltpu.VMEM(halo, BF16)] * 4
        + [
            pltpu.VMEM((2, TAPS, TAPS), BF16),
            pltpu.VMEM((tp_size, GROUPS // tp_size, TAPS), BF16),
            pltpu.VMEM((tp_size, channels // TAPS, TAPS), jnp.int32),
            pltpu.VMEM((runs, TAPS), F32),
            pltpu.VMEM((GROUPS // tp_size, GROUPS), BF16),
            pltpu.VMEM((runs * 8, TAPS), F32),
            pltpu.VMEM((runs, TAPS), F32),
            pltpu.VMEM((half, TAPS), F32),
            pltpu.VMEM((ny, half, TAPS), F32),
            pltpu.VMEM((nx, half, TAPS), F32),
            pltpu.VMEM((tp_size, 2, half, TAPS), F32),
            pltpu.VMEM((GROUPS // tp_size, TAPS), F32),
            pltpu.VMEM((2, GROUPS // tp_size // 2, TAPS), F32),
            dma((4, 4)), dma((4, CHUNKS)), dma((2, CHUNKS)), dma((2, CHUNKS)), dma((2, tp_size - 1)), dma((2, tp_size - 1)),
            pltpu.SemaphoreType.REGULAR((3,)), dma, dma, dma((ny - 1,)), dma((ny - 1,)), dma((nx - 1,)), dma((nx - 1,)),
            dma((2 * tp_size - 1,)), dma((2 * tp_size - 1,)), dma, dma,
        ],
        compiler_params=pltpu.CompilerParams(collective_id=0, has_side_effects=True, vmem_limit_bytes=42 << 20),
    )(filters, group_of.reshape(channels // TAPS, TAPS), queries, key_proj, value_proj, grad_output)

    def write(*refs):
        ins, outs, sem, last = refs[:5], refs[5:10], refs[10], refs[11]
        copies = [pltpu.make_async_copy(ins[4], outs[4], last)]
        part = channels // PARTS
        for w in range(windows):
            for i in range(PARTS):
                for a in range(4):
                    at = (w, pl.ds(i * part, part))
                    copies.append(pltpu.make_async_copy(ins[a].at[at], outs[a].at[at], sem.at[a, w, i]))
        for copy in copies:
            copy.start()
        for copy in copies:
            copy.wait()

    held = [pltpu.with_memory_space_constraint(r, pltpu.VMEM) for r in results]
    return pl.pallas_call(
        write,
        out_shape=[jax.ShapeDtypeStruct(big, BF16)] * 4 + [jax.ShapeDtypeStruct((GROUPS // tp_size, TAPS), F32)],
        in_specs=[resident] * 5,
        out_specs=[remote] * 5,
        scratch_shapes=[dma((4, windows, PARTS)), dma],
        compiler_params=pltpu.CompilerParams(vmem_limit_bytes=4 << 20),
    )(*held)


def solution(mesh):
    spec = P("dp", "tp", "ctx")
    nx = 4

    def call(queries, key_proj, value_proj, grad_output, filters, group_of):
        tokens = queries.shape[0] * queries.shape[2]

        def local(*args):
            return shards(*args, tokens, nx)

        return jax.shard_map(
            local,
            mesh=mesh,
            in_specs=(spec, spec, spec, spec, P("tp", None), P("tp")),
            out_specs=(spec, spec, spec, spec, P("tp", None)),
            check_vma=False,
        )(queries, key_proj, value_proj, grad_output, filters, group_of)

    return call
```

```python
import jax
import jax.numpy as jnp
from jax import lax
from jax.experimental import pallas as pl
from jax.experimental.pallas import tpu as pltpu
from jax.sharding import PartitionSpec as P

BF16 = jnp.bfloat16
F32 = jnp.float32
TAPS = 128
MEMBERS = 16
GROUPS = 512
CHUNKS = 16
EARLY = 2
LATER = 5
EDGES = (0, 1, 4, 8, 16)
PARTS = 1
STEPS = (1, 8)
MESH = pl.DeviceIdType.MESH


def aligned(index, size):
    return pl.ds(pl.multiple_of(index * size, size), size)


def shards(queries, key_proj, value_proj, grad_output, filters, group_of, tokens, nx):
    windows, channels, positions = queries.shape
    runs = channels // MEMBERS
    blocks = positions // TAPS
    width = channels // CHUNKS
    chunk_runs = width // MEMBERS
    stack = windows * MEMBERS
    half = runs // 2
    ctx_size = lax.axis_size("ctx")
    tp_size = lax.axis_size("tp")
    ny = ctx_size // nx
    scale_by = 1.0 / tokens

    def body(
        filt_ref, grp_ref, q_hbm, k_hbm, v_hbm, g_hbm,
        gated, gradq, gradk, gradv, gradf,
        q, k, v, g, u_out, d_out, u_in, d_in, masks, table, groups, taps_of, routes,
        partial, local, core_in, y_all, x_all, z_all, routed, both,
        edge_sem, rest_sem, halo_send, halo_recv, table_send, table_recv,
        known, core_send, core_recv, y_send, y_recv, x_send, x_recv, z_send, z_recv, last_send, last_recv,
    ):
        dp = lax.axis_index("dp")
        ctx = lax.axis_index("ctx")
        tp = lax.axis_index("tp")
        y = ctx // nx
        x = lax.rem(ctx, nx)
        after = {"ctx": lax.rem(ctx + 1, ctx_size)}
        before = {"ctx": lax.rem(ctx + ctx_size - 1, ctx_size)}
        other = {"dp": 1 - dp}
        y_peers = [{"ctx": lax.rem(y + i, ny) * nx + x} for i in range(1, ny)]
        x_peers = [{"ctx": y * nx + lax.rem(x + i, nx)} for i in range(1, nx)]
        z_peers = [{"tp": lax.rem(tp + i, tp_size)} for i in range(1, tp_size)]
        last_peers = [other] + z_peers + [{"dp": 1 - dp, **peer} for peer in z_peers]
        greeted = [after, before, other] + z_peers
        barrier = pltpu.get_barrier_semaphore()
        for peer in greeted:
            pl.semaphore_signal(barrier, 1, device_id=peer, device_id_type=MESH)

        def along(distance):
            return {"ctx": lax.rem(ctx + distance + ctx_size, ctx_size)}

        def pass_on(round_of, to):
            for peer in to:
                pl.semaphore_signal(known.at[round_of], 1, device_id=peer, device_id_type=MESH)

        hbm = [k_hbm, v_hbm, q_hbm, g_hbm]
        vmem = [k, v, q, g]
        edge_lane = [positions - TAPS, positions - TAPS, 0, 0]
        rest_lane = [0, 0, TAPS, TAPS]
        pieces = len(EDGES) - 1

        def edge_rows(a, p):
            low, high = EDGES[p] * width, EDGES[p + 1] * width
            return pl.ds(low, high - low) if a < 2 else pl.ds(channels - high, high - low)

        def edge_copy(a, p):
            part = (slice(None), edge_rows(a, p), pl.ds(edge_lane[a], TAPS))
            return pltpu.make_async_copy(hbm[a].at[part], vmem[a].at[part], edge_sem.at[a, p])

        def rest_copy(a, c):
            part = (slice(None), aligned(c, width), pl.ds(rest_lane[a], positions - TAPS))
            return pltpu.make_async_copy(hbm[a].at[part], vmem[a].at[part], rest_sem.at[a, c])

        for p in range(pieces):
            for a in range(4):
                edge_copy(a, p).start()

        def start_rest(i, carry):
            for a in range(4):
                rest_copy(a, i).start()
                rest_copy(a, CHUNKS - 1 - i).start()
            return carry

        def u_copy(c):
            part = (slice(None), aligned(c, width), slice(None))
            return pltpu.make_async_remote_copy(
                u_out.at[part], u_in.at[part], halo_send.at[0, c], halo_recv.at[0, c],
                device_id=after, device_id_type=MESH,
            )

        def d_copy(c):
            part = (slice(None), aligned(c, width), slice(None))
            return pltpu.make_async_remote_copy(
                d_out.at[part], d_in.at[part], halo_send.at[1, c], halo_recv.at[1, c],
                device_id=before, device_id_type=MESH,
            )

        not_first = ctx > 0
        not_last = ctx < ctx_size - 1

        def start_halo(i, carry):
            @pl.when(not_last)
            def _():
                u_copy(i).start()

            @pl.when(not_first)
            def _():
                d_copy(CHUNKS - 1 - i).start()

            return carry

        def halo_here(step):
            @pl.when(not_first)
            def _():
                u_copy(step).wait_recv()

            @pl.when(not_last)
            def _():
                d_copy(CHUNKS - 1 - step).wait_recv()

        def table_copies(i):
            return [
                pltpu.make_async_remote_copy(
                    ref.at[tp], ref.at[tp], table_send.at[j, i], table_recv.at[j, i],
                    device_id=z_peers[i], device_id_type=MESH,
                )
                for j, ref in enumerate((table, groups))
            ]

        @pl.when(ctx == 0)
        def _():
            u_in[...] = jnp.zeros_like(u_in)

        @pl.when(ctx == ctx_size - 1)
        def _():
            d_in[...] = jnp.zeros_like(d_in)

        for p in range(pieces):
            edge_copy(0, p).wait()
            edge_copy(1, p).wait()
            ch, ln = edge_rows(0, p), pl.ds(positions - TAPS, TAPS)
            u_out[:, ch, :] = k[:, ch, ln] * v[:, ch, ln]
            edge_copy(2, p).wait()
            edge_copy(3, p).wait()
            ch, ln = edge_rows(2, p), pl.ds(0, TAPS)
            d_out[:, ch, :] = q[:, ch, ln] * g[:, ch, ln]
            if p == 0:
                pl.semaphore_wait(barrier, len(greeted))
            lax.fori_loop(EDGES[p], EDGES[p + 1], start_halo, 0)
            if p == 0:
                table[tp] = filt_ref[...].astype(BF16)
                groups[tp] = grp_ref[...]
                for i in range(tp_size - 1):
                    for copy in table_copies(i):
                        copy.start()
                pass_on(0, [after, before, other])
            if p == 1:
                lax.fori_loop(0, CHUNKS // 2, start_rest, 0)

        row = lax.broadcasted_iota(jnp.int32, (TAPS, TAPS), 0)
        lane = lax.broadcasted_iota(jnp.int32, (TAPS, TAPS), 1)
        masks[0] = jnp.where(lane >= row, 1.0, 0.0).astype(BF16)
        masks[1] = jnp.where(lane < row, 1.0, 0.0).astype(BF16)

        nothing = jnp.zeros((stack, TAPS), BF16)

        def run_rows(ref, r, b):
            return jnp.concatenate(
                [ref[w, aligned(r, MEMBERS), TAPS * b : TAPS * b + TAPS] for w in range(windows)], axis=0
            )

        def product(left, right, r):
            return [run_rows(left, r, b) * run_rows(right, r, b) for b in range(blocks)]

        def put(out, gate, r, value):
            for b in range(blocks):
                for w in range(windows):
                    at = (w, aligned(r, MEMBERS), slice(TAPS * b, TAPS * b + TAPS))
                    first = b * stack + w * MEMBERS
                    out[at] = (gate[at].astype(F32) * value[first : first + MEMBERS]).astype(BF16)

        def circulant(r):
            rows = jnp.broadcast_to(taps_of[pl.ds(r, 1), :], (TAPS, TAPS))
            return pltpu.roll(rows, 0, 1, stride=1, stride_axis=0).astype(BF16)

        def outer(u_four, d_four, r):
            left = jnp.concatenate(u_four, axis=0)
            shifted = [nothing] + d_four
            right = jnp.concatenate(
                [jnp.concatenate([shifted[i + 1], shifted[i]], axis=1) for i in range(blocks + 1)], axis=0
            )
            pairs = lax.dot_general(left, right, (((0,), (0,)), ((), ())), preferred_element_type=F32)
            folded = jnp.where(lane >= row, pairs[:, TAPS:], pairs[:, :TAPS])
            total = folded[0:8]
            for i in range(1, TAPS // 8):
                total = total + pltpu.roll(folded[8 * i : 8 * i + 8], TAPS - 8 * i, 1)
            partial[aligned(r, 8), :] = total

        def forward(r):
            circ = circulant(r)
            u_four = [run_rows(u_in, r, 0)] + product(k, v, r)
            weights = jnp.concatenate([circ * masks[1], circ * masks[0]], axis=0)
            left = jnp.concatenate(
                [jnp.concatenate([u_four[b], u_four[b + 1]], axis=1) for b in range(blocks)], axis=0
            )
            mixed = jnp.dot(left, weights, preferred_element_type=F32)
            put(gated, q, r, mixed)
            put(gradq, g, r, mixed)

        def backward(r):
            circ = circulant(r)
            d_four = product(g, q, r) + [run_rows(d_in, r, 0)]
            weights = jnp.concatenate([circ * masks[0], circ * masks[1]], axis=1)
            left = jnp.concatenate(
                [jnp.concatenate([d_four[b], d_four[b + 1]], axis=1) for b in range(blocks)], axis=0
            )
            upward = lax.dot_general(left, weights, (((1,), (1,)), ((), ())), preferred_element_type=F32)
            put(gradk, v, r, upward)
            put(gradv, k, r, upward)

        unroll = 8

        def first_phase(step, carry):
            back = CHUNKS - 1 - step
            for a in range(4):
                rest_copy(a, step).wait()
                rest_copy(a, back).wait()
            halo_here(step)

            def some(i, inner):
                for j in range(unroll):
                    r = step * chunk_runs + i * unroll + j
                    outer([run_rows(u_in, r, 0)] + product(k, v, r), product(g, q, r) + [nothing], r)
                    r = back * chunk_runs + i * unroll + j
                    outer([nothing] + product(k, v, r), product(g, q, r) + [run_rows(d_in, r, 0)], r)
                return inner

            lax.fori_loop(0, chunk_runs // unroll, some, 0)
            for c in (step, back):
                first = pl.multiple_of(c * chunk_runs * 8, chunk_runs * 8)
                total = partial[pl.ds(first, chunk_runs, stride=8), :]
                for s in range(1, 8):
                    total = total + pltpu.roll(partial[pl.ds(first + s, chunk_runs, stride=8), :], TAPS - s, 1)
                local[aligned(c, chunk_runs), :] = total
            return carry

        middle = CHUNKS // 2
        lax.fori_loop(0, EARLY, first_phase, 0)

        pl.semaphore_wait(known.at[0], 3)
        pass_on(1, [along(2), along(-2)])
        for i in range(tp_size - 1):
            for copy in table_copies(i):
                copy.wait()

        def run_groups(z):
            ids = groups[z]
            span = TAPS // MEMBERS
            pick = jnp.where(
                lax.broadcasted_iota(jnp.int32, (runs, channels // TAPS), 1)
                == lax.broadcasted_iota(jnp.int32, (runs, channels // TAPS), 0) // span,
                1.0, 0.0,
            ).astype(BF16)
            high = jnp.dot(pick, (ids >> 4).astype(F32).astype(BF16), preferred_element_type=F32)
            low = jnp.dot(pick, (ids & 15).astype(F32).astype(BF16), preferred_element_type=F32)
            r = lax.broadcasted_iota(jnp.int32, (runs, TAPS), 0)
            l = lax.broadcasted_iota(jnp.int32, (runs, TAPS), 1)
            keep = jnp.where(l == (r % span) * MEMBERS, high * 16.0 + low, 0.0)
            return jnp.sum(keep, axis=1, keepdims=True)

        mine = run_groups(tp)
        rows_here = GROUPS // tp_size
        chosen = jnp.zeros((runs, TAPS), F32)
        for z in range(tp_size):
            ids = lax.broadcasted_iota(jnp.int32, (runs, rows_here), 1) + z * rows_here
            onehot = jnp.where(ids.astype(F32) == mine, 1.0, 0.0).astype(BF16)
            chosen = chosen + jnp.dot(onehot, table[z], preferred_element_type=F32)
        taps_of[...] = chosen
        first_row = tp * rows_here
        for z in range(tp_size):
            ids = lax.broadcasted_iota(jnp.int32, (runs, rows_here), 1) + first_row
            onehot = jnp.where(ids.astype(F32) == run_groups(z), 1.0, 0.0)
            routes[:, runs * z : runs * (z + 1)] = onehot.T.astype(BF16)

        lax.fori_loop(EARLY, LATER, first_phase, 0)
        pl.semaphore_wait(known.at[1], 2)
        pass_on(2, [along(4), along(-4)])
        lax.fori_loop(LATER, middle, first_phase, 0)
        pl.semaphore_wait(known.at[2], 2)

        def second_phase(step, carry):
            back = CHUNKS - 1 - step

            @pl.when(step >= middle)
            def _():
                halo_here(step)

            def some(i, inner):
                for j in range(unroll):
                    forward(step * chunk_runs + i * unroll + j)
                    backward(back * chunk_runs + i * unroll + j)
                return inner

            return lax.fori_loop(0, chunk_runs // unroll, some, carry)

        own = aligned(dp, half)
        theirs = aligned(1 - dp, half)
        core_copy = pltpu.make_async_remote_copy(
            local.at[theirs], core_in, core_send, core_recv, device_id=other, device_id_type=MESH
        )
        core_copy.start()
        def finish(i, carry):
            @pl.when(not_last)
            def _():
                u_copy(i).wait_send()

            @pl.when(not_first)
            def _():
                d_copy(i).wait_send()

            return carry

        lax.fori_loop(0, STEPS[0], second_phase, 0)

        def spread(ref, slot, send, recv, to):
            copies = [
                pltpu.make_async_remote_copy(
                    ref.at[slot], ref.at[slot], send.at[i], recv.at[i], device_id=peer, device_id_type=MESH
                )
                for i, peer in enumerate(to)
            ]
            for copy in copies:
                copy.start()
            return copies

        def summed(ref, count):
            result = ref[0]
            for i in range(1, count):
                result = result + ref[i]
            return result

        core_copy.wait()
        z_all[tp, dp] = local[own, :] + core_in[...]
        z_copies = spread(z_all, (tp, dp), z_send, z_recv, last_peers)
        lax.fori_loop(STEPS[0], STEPS[1], second_phase, 0)
        for copy in z_copies:
            copy.wait()
        rest = jnp.concatenate([z_all[z, core] for z in range(tp_size) for core in range(2)], axis=0)
        result = jnp.zeros((rows_here, TAPS), F32)
        for _ in range(3):
            piece_of = rest.astype(BF16)
            rest = rest - piece_of.astype(F32)
            result = result + jnp.dot(routes[...], piece_of, preferred_element_type=F32)
        routed[...] = result * scale_by
        x_all[x] = routed[own, :]
        x_copies = spread(x_all, x, x_send, x_recv, x_peers)
        lax.fori_loop(STEPS[1], CHUNKS, second_phase, 0)
        for copy in x_copies:
            copy.wait()
        y_all[y] = summed(x_all, nx)
        y_copies = spread(y_all, y, y_send, y_recv, y_peers)
        lax.fori_loop(0, CHUNKS, finish, 0)
        for copy in y_copies:
            copy.wait()
        both[dp] = summed(y_all, ny)
        last_copy = pltpu.make_async_remote_copy(
            both.at[dp], both.at[dp], last_send, last_recv, device_id=other, device_id_type=MESH
        )
        last_copy.start()
        last_copy.wait()
        gradf[: rows_here // 2, :] = both[0]
        gradf[rows_here // 2 :, :] = both[1]


    resident = pl.BlockSpec(memory_space=pltpu.VMEM)
    remote = pl.BlockSpec(memory_space=pltpu.HBM)
    big = (windows, channels, positions)
    halo = (windows, channels, TAPS)
    dma = pltpu.SemaphoreType.DMA
    results = pl.pallas_call(
        body,
        out_shape=[pltpu.VMEM(big, BF16)] * 4 + [pltpu.VMEM((GROUPS // tp_size, TAPS), F32)],
        in_specs=[resident, resident] + [remote] * 4,
        out_specs=[resident] * 5,
        scratch_shapes=[pltpu.VMEM(big, BF16)] * 4
        + [pltpu.VMEM(halo, BF16)] * 4
        + [
            pltpu.VMEM((2, TAPS, TAPS), BF16),
            pltpu.VMEM((tp_size, GROUPS // tp_size, TAPS), BF16),
            pltpu.VMEM((tp_size, channels // TAPS, TAPS), jnp.int32),
            pltpu.VMEM((runs, TAPS), F32),
            pltpu.VMEM((GROUPS // tp_size, GROUPS), BF16),
            pltpu.VMEM((runs * 8, TAPS), F32),
            pltpu.VMEM((runs, TAPS), F32),
            pltpu.VMEM((half, TAPS), F32),
            pltpu.VMEM((ny, half, TAPS), F32),
            pltpu.VMEM((nx, half, TAPS), F32),
            pltpu.VMEM((tp_size, 2, half, TAPS), F32),
            pltpu.VMEM((GROUPS // tp_size, TAPS), F32),
            pltpu.VMEM((2, GROUPS // tp_size // 2, TAPS), F32),
            dma((4, 4)), dma((4, CHUNKS)), dma((2, CHUNKS)), dma((2, CHUNKS)), dma((2, tp_size - 1)), dma((2, tp_size - 1)),
            pltpu.SemaphoreType.REGULAR((3,)), dma, dma, dma((ny - 1,)), dma((ny - 1,)), dma((nx - 1,)), dma((nx - 1,)),
            dma((2 * tp_size - 1,)), dma((2 * tp_size - 1,)), dma, dma,
        ],
        compiler_params=pltpu.CompilerParams(collective_id=0, has_side_effects=True, vmem_limit_bytes=42 << 20),
    )(filters, group_of.reshape(channels // TAPS, TAPS), queries, key_proj, value_proj, grad_output)

    def write(*refs):
        ins, outs, sem, last = refs[:5], refs[5:10], refs[10], refs[11]
        copies = [pltpu.make_async_copy(ins[4], outs[4], last)]
        part = channels // PARTS
        for w in range(windows):
            for i in range(PARTS):
                for a in range(4):
                    at = (w, pl.ds(i * part, part))
                    copies.append(pltpu.make_async_copy(ins[a].at[at], outs[a].at[at], sem.at[a, w, i]))
        for copy in copies:
            copy.start()
        for copy in copies:
            copy.wait()

    held = [pltpu.with_memory_space_constraint(r, pltpu.VMEM) for r in results]
    return pl.pallas_call(
        write,
        out_shape=[jax.ShapeDtypeStruct(big, BF16)] * 4 + [jax.ShapeDtypeStruct((GROUPS // tp_size, TAPS), F32)],
        in_specs=[resident] * 5,
        out_specs=[remote] * 5,
        scratch_shapes=[dma((4, windows, PARTS)), dma],
        compiler_params=pltpu.CompilerParams(vmem_limit_bytes=4 << 20),
    )(*held)


def solution(mesh):
    spec = P("dp", "tp", "ctx")
    nx = 4

    def call(queries, key_proj, value_proj, grad_output, filters, group_of):
        tokens = queries.shape[0] * queries.shape[2]

        def local(*args):
            return shards(*args, tokens, nx)

        return jax.shard_map(
            local,
            mesh=mesh,
            in_specs=(spec, spec, spec, spec, P("tp", None), P("tp")),
            out_specs=(spec, spec, spec, spec, P("tp", None)),
            check_vma=False,
        )(queries, key_proj, value_proj, grad_output, filters, group_of)

    return call
```

```python
import jax
import jax.numpy as jnp
from jax import lax
from jax.experimental import pallas as pl
from jax.experimental.pallas import tpu as pltpu
from jax.sharding import PartitionSpec as P

BF16 = jnp.bfloat16
F32 = jnp.float32
TAPS = 128
MEMBERS = 16
GROUPS = 512
CHUNKS = 16
EARLY = 2
LATER = 5
EDGES = (0, 1, 4, 8, 16)
UNROLL = (8, 8)
MESH = pl.DeviceIdType.MESH


def aligned(index, size):
    return pl.ds(pl.multiple_of(index * size, size), size)


def shards(queries, key_proj, value_proj, grad_output, filters, group_of, tokens, nx):
    windows, channels, positions = queries.shape
    runs = channels // MEMBERS
    blocks = positions // TAPS
    width = channels // CHUNKS
    chunk_runs = width // MEMBERS
    stack = windows * MEMBERS
    half = runs // 2
    ctx_size = lax.axis_size("ctx")
    tp_size = lax.axis_size("tp")
    ny = ctx_size // nx
    scale_by = 1.0 / tokens

    def body(
        filt_ref, grp_ref, q_hbm, k_hbm, v_hbm, g_hbm,
        gated, gradq, gradk, gradv, gradf,
        q, k, v, g, u_out, d_out, u_in, d_in, circs, masks, table, groups, taps_of, routes,
        partial, local, core_in, y_all, x_all, z_all, routed, both,
        edge_sem, rest_sem, halo_send, halo_recv, table_send, table_recv,
        known, core_send, core_recv, y_send, y_recv, x_send, x_recv, z_send, z_recv, last_send, last_recv,
    ):
        dp = lax.axis_index("dp")
        ctx = lax.axis_index("ctx")
        tp = lax.axis_index("tp")
        y = ctx // nx
        x = lax.rem(ctx, nx)
        after = {"ctx": lax.rem(ctx + 1, ctx_size)}
        before = {"ctx": lax.rem(ctx + ctx_size - 1, ctx_size)}
        other = {"dp": 1 - dp}
        y_peers = [{"ctx": lax.rem(y + i, ny) * nx + x} for i in range(1, ny)]
        x_peers = [{"ctx": y * nx + lax.rem(x + i, nx)} for i in range(1, nx)]
        z_peers = [{"tp": lax.rem(tp + i, tp_size)} for i in range(1, tp_size)]
        last_peers = [other] + z_peers + [{"dp": 1 - dp, **peer} for peer in z_peers]
        greeted = [after, before, other] + z_peers
        barrier = pltpu.get_barrier_semaphore()
        for peer in greeted:
            pl.semaphore_signal(barrier, 1, device_id=peer, device_id_type=MESH)

        def along(distance):
            return {"ctx": lax.rem(ctx + distance + ctx_size, ctx_size)}

        def pass_on(round_of, to):
            for peer in to:
                pl.semaphore_signal(known.at[round_of], 1, device_id=peer, device_id_type=MESH)

        hbm = [k_hbm, v_hbm, q_hbm, g_hbm]
        vmem = [k, v, q, g]
        edge_lane = [positions - TAPS, positions - TAPS, 0, 0]
        rest_lane = [0, 0, TAPS, TAPS]
        pieces = len(EDGES) - 1

        def edge_rows(a, p):
            low, high = EDGES[p] * width, EDGES[p + 1] * width
            return pl.ds(low, high - low) if a < 2 else pl.ds(channels - high, high - low)

        def edge_copy(a, p):
            part = (slice(None), edge_rows(a, p), pl.ds(edge_lane[a], TAPS))
            return pltpu.make_async_copy(hbm[a].at[part], vmem[a].at[part], edge_sem.at[a, p])

        def rest_copy(a, c):
            part = (slice(None), aligned(c, width), pl.ds(rest_lane[a], positions - TAPS))
            return pltpu.make_async_copy(hbm[a].at[part], vmem[a].at[part], rest_sem.at[a, c])

        for p in range(pieces):
            for a in range(4):
                edge_copy(a, p).start()

        def start_rest(i, carry):
            for a in range(4):
                rest_copy(a, i).start()
                rest_copy(a, CHUNKS - 1 - i).start()
            return carry

        def u_copy(c):
            part = (slice(None), aligned(c, width), slice(None))
            return pltpu.make_async_remote_copy(
                u_out.at[part], u_in.at[part], halo_send.at[0, c], halo_recv.at[0, c],
                device_id=after, device_id_type=MESH,
            )

        def d_copy(c):
            part = (slice(None), aligned(c, width), slice(None))
            return pltpu.make_async_remote_copy(
                d_out.at[part], d_in.at[part], halo_send.at[1, c], halo_recv.at[1, c],
                device_id=before, device_id_type=MESH,
            )

        not_first = ctx > 0
        not_last = ctx < ctx_size - 1

        def start_halo(i, carry):
            @pl.when(not_last)
            def _():
                u_copy(i).start()

            @pl.when(not_first)
            def _():
                d_copy(CHUNKS - 1 - i).start()

            return carry

        def halo_here(step):
            @pl.when(not_first)
            def _():
                u_copy(step).wait_recv()

            @pl.when(not_last)
            def _():
                d_copy(CHUNKS - 1 - step).wait_recv()

        def table_copies(i):
            return [
                pltpu.make_async_remote_copy(
                    ref.at[tp], ref.at[tp], table_send.at[j, i], table_recv.at[j, i],
                    device_id=z_peers[i], device_id_type=MESH,
                )
                for j, ref in enumerate((table, groups))
            ]

        @pl.when(ctx == 0)
        def _():
            u_in[...] = jnp.zeros_like(u_in)

        @pl.when(ctx == ctx_size - 1)
        def _():
            d_in[...] = jnp.zeros_like(d_in)

        for p in range(pieces):
            edge_copy(0, p).wait()
            edge_copy(1, p).wait()
            ch, ln = edge_rows(0, p), pl.ds(positions - TAPS, TAPS)
            u_out[:, ch, :] = k[:, ch, ln] * v[:, ch, ln]
            edge_copy(2, p).wait()
            edge_copy(3, p).wait()
            ch, ln = edge_rows(2, p), pl.ds(0, TAPS)
            d_out[:, ch, :] = q[:, ch, ln] * g[:, ch, ln]
            if p == 0:
                pl.semaphore_wait(barrier, len(greeted))
            lax.fori_loop(EDGES[p], EDGES[p + 1], start_halo, 0)
            if p == 0:
                table[tp] = filt_ref[...].astype(BF16)
                groups[tp] = grp_ref[...]
                for i in range(tp_size - 1):
                    for copy in table_copies(i):
                        copy.start()
                pass_on(0, [after, before, other])
            if p == 1:
                lax.fori_loop(0, CHUNKS // 2, start_rest, 0)

        row = lax.broadcasted_iota(jnp.int32, (TAPS, TAPS), 0)
        lane = lax.broadcasted_iota(jnp.int32, (TAPS, TAPS), 1)
        masks[0] = jnp.where(lane >= row, 1.0, 0.0).astype(BF16)
        masks[1] = jnp.where(lane < row, 1.0, 0.0).astype(BF16)

        nothing = jnp.zeros((stack, TAPS), BF16)

        def run_rows(ref, r, b):
            return jnp.concatenate(
                [ref[w, aligned(r, MEMBERS), TAPS * b : TAPS * b + TAPS] for w in range(windows)], axis=0
            )

        def product(left, right, r):
            return [run_rows(left, r, b) * run_rows(right, r, b) for b in range(blocks)]

        def put(out, gate, r, value):
            for b in range(blocks):
                for w in range(windows):
                    at = (w, aligned(r, MEMBERS), slice(TAPS * b, TAPS * b + TAPS))
                    first = b * stack + w * MEMBERS
                    out[at] = (gate[at].astype(F32) * value[first : first + MEMBERS]).astype(BF16)

        def circulant(r):
            rows = jnp.broadcast_to(taps_of[pl.ds(r, 1), :], (TAPS, TAPS))
            made = pltpu.roll(rows, 0, 1, stride=1, stride_axis=0).astype(BF16)
            circs[r] = made
            return made

        def outer(u_four, d_four, r):
            left = jnp.concatenate(u_four, axis=0)
            shifted = [nothing] + d_four
            right = jnp.concatenate(
                [jnp.concatenate([shifted[i + 1], shifted[i]], axis=1) for i in range(blocks + 1)], axis=0
            )
            pairs = lax.dot_general(left, right, (((0,), (0,)), ((), ())), preferred_element_type=F32)
            folded = jnp.where(lane >= row, pairs[:, TAPS:], pairs[:, :TAPS])
            total = folded[0:8]
            for i in range(1, TAPS // 8):
                total = total + pltpu.roll(folded[8 * i : 8 * i + 8], TAPS - 8 * i, 1)
            partial[aligned(r, 8), :] = total

        def forward(r, circ):
            u_four = [run_rows(u_in, r, 0)] + product(k, v, r)
            weights = jnp.concatenate([circ * masks[1], circ * masks[0]], axis=0)
            left = jnp.concatenate(
                [jnp.concatenate([u_four[b], u_four[b + 1]], axis=1) for b in range(blocks)], axis=0
            )
            mixed = jnp.dot(left, weights, preferred_element_type=F32)
            put(gated, q, r, mixed)
            put(gradq, g, r, mixed)

        def backward(r, circ):
            d_four = product(g, q, r) + [run_rows(d_in, r, 0)]
            weights = jnp.concatenate([circ * masks[0], circ * masks[1]], axis=1)
            left = jnp.concatenate(
                [jnp.concatenate([d_four[b], d_four[b + 1]], axis=1) for b in range(blocks)], axis=0
            )
            upward = lax.dot_general(left, weights, (((1,), (1,)), ((), ())), preferred_element_type=F32)
            put(gradk, v, r, upward)
            put(gradv, k, r, upward)

        def gradient(step, also):
            back = CHUNKS - 1 - step
            for a in range(4):
                rest_copy(a, step).wait()
                rest_copy(a, back).wait()
            halo_here(step)

            def some(i, inner):
                for j in range(UNROLL[0]):
                    r = step * chunk_runs + i * UNROLL[0] + j
                    outer([run_rows(u_in, r, 0)] + product(k, v, r), product(g, q, r) + [nothing], r)
                    if also:
                        forward(r, circulant(r))
                    r = back * chunk_runs + i * UNROLL[0] + j
                    outer([nothing] + product(k, v, r), product(g, q, r) + [run_rows(d_in, r, 0)], r)
                    if also:
                        backward(r, circulant(r))
                return inner

            lax.fori_loop(0, chunk_runs // UNROLL[0], some, 0)
            for c in (step, back):
                first = pl.multiple_of(c * chunk_runs * 8, chunk_runs * 8)
                total = partial[pl.ds(first, chunk_runs, stride=8), :]
                for s in range(1, 8):
                    total = total + pltpu.roll(partial[pl.ds(first + s, chunk_runs, stride=8), :], TAPS - s, 1)
                local[aligned(c, chunk_runs), :] = total

        def gradient_alone(step, carry):
            gradient(step, False)
            return carry

        def gradient_and_more(step, carry):
            gradient(step, True)
            return carry

        middle = CHUNKS // 2

        def convolve(step, carry, made):
            back = CHUNKS - 1 - step

            def some(i, inner):
                for j in range(UNROLL[1]):
                    r = step * chunk_runs + i * UNROLL[1] + j
                    forward(r, circs[r] if made else circulant(r))
                    r = back * chunk_runs + i * UNROLL[1] + j
                    backward(r, circs[r] if made else circulant(r))
                return inner

            return lax.fori_loop(0, chunk_runs // UNROLL[1], some, carry)

        def left_over(step, carry):
            return convolve(step, carry, False)

        def second_phase(step, carry):
            halo_here(step)
            return convolve(step, carry, True)

        lax.fori_loop(0, EARLY, gradient_alone, 0)

        pl.semaphore_wait(known.at[0], 3)
        pass_on(1, [along(2), along(-2)])
        for i in range(tp_size - 1):
            for copy in table_copies(i):
                copy.wait()

        def run_groups(z):
            ids = groups[z]
            span = TAPS // MEMBERS
            pick = jnp.where(
                lax.broadcasted_iota(jnp.int32, (runs, channels // TAPS), 1)
                == lax.broadcasted_iota(jnp.int32, (runs, channels // TAPS), 0) // span,
                1.0, 0.0,
            ).astype(BF16)
            high = jnp.dot(pick, (ids >> 4).astype(F32).astype(BF16), preferred_element_type=F32)
            low = jnp.dot(pick, (ids & 15).astype(F32).astype(BF16), preferred_element_type=F32)
            r = lax.broadcasted_iota(jnp.int32, (runs, TAPS), 0)
            l = lax.broadcasted_iota(jnp.int32, (runs, TAPS), 1)
            keep = jnp.where(l == (r % span) * MEMBERS, high * 16.0 + low, 0.0)
            return jnp.sum(keep, axis=1, keepdims=True)

        mine = run_groups(tp)
        rows_here = GROUPS // tp_size
        chosen = jnp.zeros((runs, TAPS), F32)
        for z in range(tp_size):
            ids = lax.broadcasted_iota(jnp.int32, (runs, rows_here), 1) + z * rows_here
            onehot = jnp.where(ids.astype(F32) == mine, 1.0, 0.0).astype(BF16)
            chosen = chosen + jnp.dot(onehot, table[z], preferred_element_type=F32)
        taps_of[...] = chosen
        first_row = tp * rows_here
        for z in range(tp_size):
            ids = lax.broadcasted_iota(jnp.int32, (runs, rows_here), 1) + first_row
            onehot = jnp.where(ids.astype(F32) == run_groups(z), 1.0, 0.0)
            routes[:, runs * z : runs * (z + 1)] = onehot.T.astype(BF16)

        lax.fori_loop(EARLY, LATER, gradient_and_more, 0)
        pl.semaphore_wait(known.at[1], 2)
        pass_on(2, [along(4), along(-4)])
        lax.fori_loop(LATER, middle, gradient_alone, 0)
        pl.semaphore_wait(known.at[2], 2)
        own = aligned(dp, half)
        theirs = aligned(1 - dp, half)
        core_copy = pltpu.make_async_remote_copy(
            local.at[theirs], core_in, core_send, core_recv, device_id=other, device_id_type=MESH
        )
        core_copy.start()
        def finish(i, carry):
            @pl.when(not_last)
            def _():
                u_copy(i).wait_send()

            @pl.when(not_first)
            def _():
                d_copy(i).wait_send()

            return carry

        lax.fori_loop(0, EARLY, left_over, 0)

        def spread(ref, slot, send, recv, to):
            copies = [
                pltpu.make_async_remote_copy(
                    ref.at[slot], ref.at[slot], send.at[i], recv.at[i], device_id=peer, device_id_type=MESH
                )
                for i, peer in enumerate(to)
            ]
            for copy in copies:
                copy.start()
            return copies

        def summed(ref, count):
            result = ref[0]
            for i in range(1, count):
                result = result + ref[i]
            return result

        core_copy.wait()
        z_all[tp, dp] = local[own, :] + core_in[...]
        z_copies = spread(z_all, (tp, dp), z_send, z_recv, last_peers)
        lax.fori_loop(LATER, middle, left_over, 0)
        for copy in z_copies:
            copy.wait()
        rest = jnp.concatenate([z_all[z, core] for z in range(tp_size) for core in range(2)], axis=0)
        result = jnp.zeros((rows_here, TAPS), F32)
        for _ in range(3):
            piece_of = rest.astype(BF16)
            rest = rest - piece_of.astype(F32)
            result = result + jnp.dot(routes[...], piece_of, preferred_element_type=F32)
        routed[...] = result * scale_by
        x_all[x] = routed[own, :]
        x_copies = spread(x_all, x, x_send, x_recv, x_peers)
        lax.fori_loop(middle, CHUNKS, second_phase, 0)
        for copy in x_copies:
            copy.wait()
        y_all[y] = summed(x_all, nx)
        y_copies = spread(y_all, y, y_send, y_recv, y_peers)
        lax.fori_loop(0, CHUNKS, finish, 0)
        for copy in y_copies:
            copy.wait()
        both[dp] = summed(y_all, ny)
        last_copy = pltpu.make_async_remote_copy(
            both.at[dp], both.at[dp], last_send, last_recv, device_id=other, device_id_type=MESH
        )
        last_copy.start()
        last_copy.wait()
        gradf[: rows_here // 2, :] = both[0]
        gradf[rows_here // 2 :, :] = both[1]


    resident = pl.BlockSpec(memory_space=pltpu.VMEM)
    remote = pl.BlockSpec(memory_space=pltpu.HBM)
    big = (windows, channels, positions)
    halo = (windows, channels, TAPS)
    dma = pltpu.SemaphoreType.DMA
    results = pl.pallas_call(
        body,
        out_shape=[pltpu.VMEM(big, BF16)] * 4 + [pltpu.VMEM((GROUPS // tp_size, TAPS), F32)],
        in_specs=[resident, resident] + [remote] * 4,
        out_specs=[resident] * 5,
        scratch_shapes=[pltpu.VMEM(big, BF16)] * 4
        + [pltpu.VMEM(halo, BF16)] * 4
        + [
            pltpu.VMEM((runs, TAPS, TAPS), BF16),
            pltpu.VMEM((2, TAPS, TAPS), BF16),
            pltpu.VMEM((tp_size, GROUPS // tp_size, TAPS), BF16),
            pltpu.VMEM((tp_size, channels // TAPS, TAPS), jnp.int32),
            pltpu.VMEM((runs, TAPS), F32),
            pltpu.VMEM((GROUPS // tp_size, GROUPS), BF16),
            pltpu.VMEM((runs * 8, TAPS), F32),
            pltpu.VMEM((runs, TAPS), F32),
            pltpu.VMEM((half, TAPS), F32),
            pltpu.VMEM((ny, half, TAPS), F32),
            pltpu.VMEM((nx, half, TAPS), F32),
            pltpu.VMEM((tp_size, 2, half, TAPS), F32),
            pltpu.VMEM((GROUPS // tp_size, TAPS), F32),
            pltpu.VMEM((2, GROUPS // tp_size // 2, TAPS), F32),
            dma((4, 4)), dma((4, CHUNKS)), dma((2, CHUNKS)), dma((2, CHUNKS)), dma((2, tp_size - 1)), dma((2, tp_size - 1)),
            pltpu.SemaphoreType.REGULAR((3,)), dma, dma, dma((ny - 1,)), dma((ny - 1,)), dma((nx - 1,)), dma((nx - 1,)),
            dma((2 * tp_size - 1,)), dma((2 * tp_size - 1,)), dma, dma,
        ],
        compiler_params=pltpu.CompilerParams(collective_id=0, has_side_effects=True, vmem_limit_bytes=42 << 20),
    )(filters, group_of.reshape(channels // TAPS, TAPS), queries, key_proj, value_proj, grad_output)

    def write(*refs):
        ins, outs, sem, last = refs[:5], refs[5:10], refs[10], refs[11]
        copies = [pltpu.make_async_copy(ins[4], outs[4], last)]
        copies += [pltpu.make_async_copy(ins[a], outs[a], sem.at[a]) for a in range(4)]
        for copy in copies:
            copy.start()
        for copy in copies:
            copy.wait()

    held = [pltpu.with_memory_space_constraint(r, pltpu.VMEM) for r in results]
    return pl.pallas_call(
        write,
        out_shape=[jax.ShapeDtypeStruct(big, BF16)] * 4 + [jax.ShapeDtypeStruct((GROUPS // tp_size, TAPS), F32)],
        in_specs=[resident] * 5,
        out_specs=[remote] * 5,
        scratch_shapes=[dma((4,)), dma],
        compiler_params=pltpu.CompilerParams(vmem_limit_bytes=4 << 20),
    )(*held)


def solution(mesh):
    spec = P("dp", "tp", "ctx")
    nx = 4

    def call(queries, key_proj, value_proj, grad_output, filters, group_of):
        tokens = queries.shape[0] * queries.shape[2]

        def local(*args):
            return shards(*args, tokens, nx)

        return jax.shard_map(
            local,
            mesh=mesh,
            in_specs=(spec, spec, spec, spec, P("tp", None), P("tp")),
            out_specs=(spec, spec, spec, spec, P("tp", None)),
            check_vma=False,
        )(queries, key_proj, value_proj, grad_output, filters, group_of)

    return call
```
